128 devices in a mesh: blk: 16 (over y_lo, z, core), bin: 8 (over x, y_hi).
Axes of the slice: x: 4, y: 4 (y_hi: 2, y_lo: 2; y = y_hi * 2 + y_lo), z: 4, core: 2. Of those that a mesh axis runs over, the one named last changes fastest.
Arguments:
- spectra: bfloat16 [256, 8192, 2, 128], P('bin', 'blk'), may hold values from -48 to 48
- quality: bfloat16 [256, 8192], P('bin', 'blk'), may hold values from 0 to 1
- bins: int32 [32], replicated, may hold values from 0 to 127
Outputs:
- cross: bfloat16 [4, 2, 32, 8192, 512], P(None, None, 'bin', 'blk')
The draws below stay inside these ranges and needn't reach their ends.
All inputs are finite; a program needn't handle non-finite values.
Results may differ from the reference program's by a relative error of at most 0.0057.
Values may be sent and summed in bfloat16 or wider, within the bound.
No kernel may reach another device: no remote copies, remote signals or barrier semaphores. Data moves between devices by JAX's collectives and lax.ppermute only.
A program may use at most 128 MiB of HBM per device.

```python
import math
import jax
import jax.numpy as jnp
from jax import lax

CB = 512
FB = 128
NB = 32
HALF_SPAN = 4
ROUNDS = 4
CH = 8192
WIN = 256
N_BLK = 16


def draw_spectra(key, part):
    key = jax.random.fold_in(key, 11)
    first, second, third, fourth, fifth = jax.random.split(key, 5)
    base = jnp.clip(jax.random.normal(first, (WIN, CH, 2, FB), jnp.float32), -5.0, 5.0)
    window_scale = jax.random.uniform(second, (WIN, CH, 1, 1), jnp.float32, -1.2, 1.2)
    bin_scale = jax.random.uniform(third, (1, CH, 1, FB), jnp.float32, -0.8, 0.8)
    dropout_rate = jax.random.randint(fourth, (1, CH, 1, 1), 2, 7)
    dropout_state = jax.random.randint(fifth, (WIN, CH, 1, 1), 0, 12)
    dropped = dropout_state < dropout_rate
    values = base * jnp.exp(window_scale + bin_scale)
    return jnp.where(dropped, 0.0, values).astype(jnp.bfloat16)


def draw_quality(key, part):
    key = jax.random.fold_in(key, 23)
    keys = jax.random.split(key, 12)
    run_width = 16
    groups = (CH + run_width - 1) // run_width
    shortest = max(1, WIN // 10)
    longest = max(shortest + 1, WIN // 2 + 1)
    start_one = jax.random.randint(keys[0], (1, groups), 0, WIN)
    length_one = jax.random.randint(keys[1], (1, groups), shortest, longest)
    start_two = jax.random.randint(keys[2], (1, groups), 0, WIN)
    length_two = jax.random.randint(keys[3], (1, groups), shortest, longest)
    has_one = jax.random.randint(keys[4], (1, groups), 0, 4) != 0
    has_two = jax.random.randint(keys[5], (1, groups), 0, 2) != 0
    windows = jnp.arange(WIN)[:, None]
    down_one = has_one & (windows >= start_one) & (windows < start_one + length_one)
    down_two = has_two & (windows >= start_two) & (windows < start_two + length_two)
    down = jnp.repeat(down_one | down_two, run_width, axis=1)[:, :CH]
    channel_state = jax.random.randint(keys[6], (1, CH), 0, 16)
    window_state = jax.random.randint(keys[7], (WIN, CH), 0, 16)
    alive = (channel_state != 0) & (window_state != 0) & jnp.logical_not(down)
    faint = jax.random.randint(keys[8], (1, CH), 0, 8) == 0
    strong_level = jnp.exp(jax.random.uniform(keys[9], (1, CH), jnp.float32, math.log(0.3), 0.0))
    faint_level = jnp.exp(jax.random.uniform(keys[10], (1, CH), jnp.float32, math.log(0.001), math.log(0.01)))
    level = jnp.where(faint, faint_level, strong_level)
    factor = jax.random.uniform(keys[11], (WIN, CH), jnp.float32, 0.25, 1.0)
    return jnp.where(alive, level * factor, 0.0).astype(jnp.bfloat16)


def place_ends(array, rng, least, high):
    extent = array.shape
    index_at = [jax.random.randint(jax.random.fold_in(rng, axis), (), 0, extent[axis]) for axis in range(len(extent))]
    array = array.at[tuple(index_at)].set(least)
    longest = extent.index(max(extent))
    index_at[longest] = (index_at[longest] + 1) % extent[longest]
    return array.at[tuple(index_at)].set(high)


def setup_inputs(seed: int = 0) -> dict:
    seeds = jax.random.split(jax.random.key(seed), 4)
    spectra = draw_spectra(jax.random.fold_in(seeds[3], 71), 0)
    quality = draw_quality(jax.random.fold_in(seeds[3], 71), 0)
    bins = place_ends(jax.random.randint(seeds[2], (NB,), 0, FB), jax.random.fold_in(seeds[2], 1), 0, FB - 1).astype(jnp.int32)
    return dict(spectra=spectra, quality=quality, bins=bins)


def whiten(spectra, quality, bins):
    values = spectra.astype(jnp.float32)
    power = values[:, :, 0, :] ** 2 + values[:, :, 1, :] ** 2
    offsets = jnp.arange(FB)
    band = (jnp.abs(offsets[:, None] - offsets[None, :]) <= HALF_SPAN).astype(jnp.float32)
    smooth = jnp.dot(power, band, precision=lax.Precision.HIGHEST)
    level = lax.optimization_barrier(jnp.mean(power, axis=-1, keepdims=True))
    scale = jnp.sqrt(smooth / (2 * HALF_SPAN + 1) + 0.1 * level + 1e-06)
    white = values / scale[:, :, None, :] * quality.astype(jnp.float32)[:, :, None, None]
    return jnp.take(white, bins, axis=3).astype(jnp.bfloat16)

def block_tile(items):
    own, own_weight, other, other_weight = items
    mine = own.astype(jnp.float32)
    theirs = other.astype(jnp.float32)
    left = jnp.stack([jnp.stack([mine[:, 0], mine[:, 1]], 0), jnp.stack([mine[:, 1], -mine[:, 0]], 0)], 0)
    product = jnp.einsum('opwfi,wpfk->ofik', left, theirs)
    counts = jnp.einsum('wi,wk->ik', own_weight, other_weight)
    return (product * lax.rsqrt(jnp.maximum(counts, 1.0))).astype(jnp.bfloat16)

def reference(spectra, quality, bins):
    chosen = whiten(spectra, quality, bins)
    blocks = chosen.reshape(WIN, N_BLK, CB, 2, NB).transpose(1, 0, 3, 4, 2)
    flags = quality.astype(jnp.float32).reshape(WIN, N_BLK, CB).transpose(1, 0, 2)
    results = []
    for step in range(ROUNDS):
        other = jnp.roll(blocks, -(step + 1), axis=0)
        other_weight = jnp.roll(flags, -(step + 1), axis=0)
        tiles = lax.map(block_tile, (blocks, flags, other, other_weight))
        results.append(tiles.transpose(1, 2, 0, 3, 4).reshape(2, NB, CH, CB))
    return jnp.stack(results, 0)
```

```python
import jax
import jax.numpy as jnp
from jax import lax
from jax.experimental import pallas as pl
from jax.experimental.pallas import tpu as pltpu
from jax.sharding import PartitionSpec as P

FB = 128
HALF_SPAN = 4
ROUNDS = 4
ROWS_Z = 4
WIN_STEP = 4
WIN_GROUP = 16
PIECES = 4
RELAYED = 2
MIB = 1024 * 1024


def whiten_kernel(bins_ref, x_ref, q_ref, *refs, channels, kept, shares, pieces):
    outs = refs[:pieces]
    parted, band, picker, staged = refs[pieces:]
    step = pl.program_id(0)

    @pl.when(step == 0)
    def _():
        lanes = lax.broadcasted_iota(jnp.int32, (kept, 2 * FB), 1)
        rows = lax.broadcasted_iota(jnp.int32, (kept, 2 * FB), 0)
        wanted = jnp.zeros((kept, 2 * FB), jnp.int32)
        for n in range(kept):
            wanted = jnp.where(rows == n, bins_ref[n], wanted)
        offset = jnp.where(lanes >= FB, lanes - FB, lanes)
        near = jnp.abs(offset - wanted) <= HALF_SPAN
        band[:kept] = jnp.where(near, 1.0, 0.0).astype(jnp.bfloat16)
        band[kept:] = jnp.ones((16, 2 * FB), jnp.bfloat16)
        exact = offset == wanted
        picker[:kept] = jnp.where(exact & (lanes < FB), 1.0, 0.0).astype(jnp.bfloat16)
        picker[kept:] = jnp.where(exact & (lanes >= FB), 1.0, 0.0).astype(jnp.bfloat16)

    along = (((1,), (1,)), ((), ()))
    for k in range(WIN_STEP):
        parted[k] = x_ref[k].astype(jnp.float32)
        real = parted[k, pl.ds(0, channels, stride=2), :]
        imag = parted[k, pl.ds(1, channels, stride=2), :]
        power = real * real + imag * imag
        high = power.astype(jnp.bfloat16)
        low = (power - high.astype(jnp.float32)).astype(jnp.bfloat16)
        sums = lax.dot_general(
            band[...], jnp.concatenate([high, low], 1), along, preferred_element_type=jnp.float32
        )
        both = jnp.concatenate([real.astype(jnp.bfloat16), imag.astype(jnp.bfloat16)], 1)
        picked = lax.dot_general(picker[...], both, along, preferred_element_type=jnp.float32)
        level = sums[kept:kept + 1] * (0.1 / FB) + 1e-06
        scale = lax.rsqrt(sums[:kept] * (1.0 / (2 * HALF_SPAN + 1)) + level)
        window = step * WIN_STEP + k
        gain = q_ref[pl.ds(window, 1), :] * scale
        local = lax.rem(window, WIN_GROUP)
        value = jnp.concatenate([picked[:kept] * gain, picked[kept:] * gain], 0)
        for c in range(0, channels, 128):
            staged[c // 128, pl.ds(local, 2 * kept, stride=WIN_GROUP), :] = value[:, c:c + 128]

    @pl.when(lax.rem(step, WIN_GROUP // WIN_STEP) == WIN_GROUP // WIN_STEP - 1)
    def _():
        for n in range(kept):
            share, place = n // (kept // shares), n % (kept // shares)
            for part in range(2):
                row = (part * kept + n) * WIN_GROUP
                for c in range(0, channels, 128):
                    outs[place][share, part, :, c:c + 128] = staged[c // 128, row:row + WIN_GROUP, :].astype(
                        jnp.bfloat16
                    )


def whiten(spectra, quality, bins, shares):
    windows, channels = quality.shape
    kept = bins.shape[0]
    rows = spectra.reshape(windows, channels * 2, FB)
    group = WIN_GROUP // WIN_STEP
    piece = jax.ShapeDtypeStruct((shares, 2, windows, channels), jnp.bfloat16)
    return pl.pallas_call(
        lambda *refs: whiten_kernel(*refs, channels=channels, kept=kept, shares=shares, pieces=PIECES),
        grid=(windows // WIN_STEP,),
        in_specs=[
            pl.BlockSpec(memory_space=pltpu.SMEM),
            pl.BlockSpec((WIN_STEP, channels * 2, FB), lambda i: (i, 0, 0)),
            pl.BlockSpec((windows, channels), lambda i: (0, 0)),
        ],
        out_specs=[pl.BlockSpec((shares, 2, WIN_GROUP, channels), lambda i: (0, 0, i // group, 0))] * PIECES,
        out_shape=[piece] * PIECES,
        scratch_shapes=[
            pltpu.VMEM((WIN_STEP, channels * 2, FB), jnp.float32),
            pltpu.VMEM((kept + 16, 2 * FB), jnp.bfloat16),
            pltpu.VMEM((2 * kept, 2 * FB), jnp.bfloat16),
            pltpu.VMEM((channels // 128, 2 * kept * WIN_GROUP, 128), jnp.float32),
        ],
        compiler_params=pltpu.CompilerParams(vmem_limit_bytes=40 * MIB),
        cost_estimate=pl.CostEstimate(flops=4 * 10**9, bytes_accessed=11 * 10**6, transcendentals=524288),
    )(bins, rows, quality.astype(jnp.float32))


def turn_kernel(own_ref, out_ref):
    channels = own_ref.shape[-1]
    depth = out_ref.shape[-1]
    own = own_ref[...]
    out_ref[:channels] = own.reshape(depth, channels).T
    turned = jnp.concatenate([own[:, 1:], -own[:, :1]], 1)
    out_ref[channels:] = turned.reshape(depth, channels).T


def turn(own):
    shares, _, windows, channels = own.shape
    depth = shares * 2 * windows
    return pl.pallas_call(
        turn_kernel,
        out_shape=jax.ShapeDtypeStruct((2 * channels, depth), jnp.bfloat16),
        compiler_params=pltpu.CompilerParams(vmem_limit_bytes=24 * MIB),
        cost_estimate=pl.CostEstimate(flops=0, bytes_accessed=3 * 10**6, transcendentals=0),
    )(own)


def weight_kernel(own_ref, other_ref, out_ref):
    counts = lax.dot_general(
        own_ref[...], other_ref[...], (((0,), (0,)), ((), ())), preferred_element_type=jnp.float32
    )
    out_ref[...] = lax.rsqrt(jnp.maximum(counts, 1.0))


def weights(marks):
    depth, channels = marks.shape[1:]
    return pl.pallas_call(
        weight_kernel,
        grid=(ROUNDS,),
        in_specs=[
            pl.BlockSpec((None, depth, channels), lambda r: (0, 0, 0)),
            pl.BlockSpec((None, depth, channels), lambda r: (r + 1, 0, 0)),
        ],
        out_specs=pl.BlockSpec((None, channels, channels), lambda r: (r, 0, 0)),
        out_shape=jax.ShapeDtypeStruct((ROUNDS, channels, channels), jnp.float32),
        compiler_params=pltpu.CompilerParams(vmem_limit_bytes=24 * MIB),
        cost_estimate=pl.CostEstimate(flops=5 * 10**8, bytes_accessed=5 * 10**6, transcendentals=10**6),
    )(marks, marks)


def cross_kernel(left_ref, near_ref, far_ref, weight_ref, *refs):
    out_ref = refs[-1]
    channels = out_ref.shape[-1]
    depth = left_ref.shape[-1]

    def products(other_ref):
        other = other_ref[...].reshape(depth, channels)
        for part in range(2):
            product = jnp.dot(
                left_ref[part * channels:(part + 1) * channels], other, preferred_element_type=jnp.float32
            )
            out_ref[part] = (product * weight_ref[...]).astype(jnp.bfloat16)

    @pl.when(pl.program_id(0) == 0)
    def _():
        products(near_ref)

    @pl.when(pl.program_id(0) == 1)
    def _():
        products(far_ref)


def cross(left, near, far, weight, first_round, place, held):
    depth, channels = left.shape[1], left.shape[0] // 2
    block = pl.BlockSpec(near.shape, lambda r: (0, 0, 0, 0))
    shape = jax.ShapeDtypeStruct((ROUNDS, 2, PIECES, channels, channels), jnp.bfloat16)
    extra = [] if held is None else [held]
    return pl.pallas_call(
        cross_kernel,
        grid=(2,),
        in_specs=[
            pl.BlockSpec(left.shape, lambda r: (0, 0)),
            block,
            block,
            pl.BlockSpec((None, channels, channels), lambda r: (first_round + r, 0, 0)),
        ]
        + [pl.BlockSpec(memory_space=pl.ANY)] * len(extra),
        out_specs=pl.BlockSpec((None, 2, None, channels, channels), lambda r: (first_round + r, 0, place, 0, 0)),
        out_shape=shape,
        input_output_aliases={} if held is None else {4: 0},
        compiler_params=pltpu.CompilerParams(vmem_limit_bytes=32 * MIB),
        cost_estimate=pl.CostEstimate(flops=2 * 10**9, bytes_accessed=6 * 10**6, transcendentals=0),
    )(left, near, far, weight, *extra)


def shards(spectra, quality, bins):
    blocks = lax.axis_size("blk")
    shares = lax.axis_size("bin")
    windows, channels = quality.shape
    chips = blocks // 2
    core = lax.rem(lax.axis_index("blk"), 2)

    def moved(value, pairs):
        return lax.ppermute(value, "blk", [(2 * s + c, 2 * t + c) for s, t in pairs for c in range(2)])

    def back(value):
        return moved(value, [((t + 1) % chips, t) for t in range(chips)])

    def chip(row, z):
        return (row % (chips // ROWS_Z)) * ROWS_Z + z % ROWS_Z

    every = [(row, z) for row in range(chips // ROWS_Z) for z in range(ROWS_Z)]

    def forth(value):
        return moved(value, [(chip(row, z - 1), chip(row, z)) for row, z in every])

    def forth_last(value):
        return moved(value, [(chip(row + (z + 2) // ROWS_Z, z - 1), chip(row, z)) for row, z in every])

    def swapped(value):
        return lax.ppermute(value, "blk", [(i, i ^ 1) for i in range(blocks)])

    def shifted(value, steps):
        return lax.ppermute(value, "blk", [((i + steps) % blocks, i) for i in range(blocks)])

    marks = jnp.stack([quality] + [shifted(quality, r + 1) for r in range(ROUNDS)], 0)
    marks = lax.all_gather(marks, "bin", axis=0, tiled=False)
    marks = marks.transpose(1, 0, 2, 3).reshape(ROUNDS + 1, shares * windows, channels)
    weight = weights(marks)

    sent = whiten(spectra, quality, bins, shares)
    own = [lax.all_to_all(value, "bin", split_axis=0, concat_axis=0, tiled=True) for value in sent]
    out = None
    near = [back(value) for value in own]
    left = [turn(value) for value in own]
    far = [
        back(near[place]) if place < RELAYED else forth_last(forth(own[place])) for place in range(PIECES)
    ]
    for place in range(PIECES):
        first = swapped(jnp.where(core == 1, own[place], near[place]))
        out = cross(left[place], first, near[place], weight, 0, place, out)
    for place in range(PIECES):
        third = swapped(jnp.where(core == 1, near[place], far[place]))
        out = cross(left[place], third, far[place], weight, 2, place, out)
    return out


def solution(mesh):
    return jax.shard_map(
        shards,
        mesh=mesh,
        in_specs=(P("bin", "blk", None, None), P("bin", "blk"), P()),
        out_specs=P(None, None, "bin", "blk", None),
        check_vma=False,
    )
```

```python
import jax
import jax.numpy as jnp
from jax import lax
from jax.experimental import pallas as pl
from jax.experimental.pallas import tpu as pltpu
from jax.sharding import PartitionSpec as P

FB = 128
HALF_SPAN = 4
ROUNDS = 4
ROWS_Z = 4
WIN_STEP = 8
WIN_GROUP = 16
PIECES = 2
CHUNKS = 2
MIB = 1024 * 1024
COST = 1000


def taking(micros):
    return pl.CostEstimate(flops=int(micros * COST), bytes_accessed=1000, transcendentals=0)


def whiten_kernel(bins_ref, x_ref, q_ref, *refs, channels, kept, shares, pieces):
    outs = refs[:pieces]
    parted, band, picker, staged, quality = refs[pieces:]
    depth = kept // shares // pieces
    step = pl.program_id(0)
    group = pl.multiple_of(step * WIN_STEP // WIN_GROUP * WIN_GROUP, WIN_GROUP)

    @pl.when(step == 0)
    def _():
        quality[...] = q_ref[...].astype(jnp.float32)
        lanes = lax.broadcasted_iota(jnp.int32, (kept, 2 * FB), 1)
        rows = lax.broadcasted_iota(jnp.int32, (kept, 2 * FB), 0)
        wanted = jnp.zeros((kept, 2 * FB), jnp.int32)
        for n in range(kept):
            wanted = jnp.where(rows == n, bins_ref[n], wanted)
        offset = jnp.where(lanes >= FB, lanes - FB, lanes)
        near = jnp.abs(offset - wanted) <= HALF_SPAN
        band[:kept] = jnp.where(near, 1.0, 0.0).astype(jnp.bfloat16)
        band[kept:] = jnp.ones((16, 2 * FB), jnp.bfloat16)
        exact = offset == wanted
        picker[:kept] = jnp.where(exact & (lanes < FB), 1.0, 0.0).astype(jnp.bfloat16)
        picker[kept:] = jnp.where(exact & (lanes >= FB), 1.0, 0.0).astype(jnp.bfloat16)

    along = (((1,), (1,)), ((), ()))
    for k in range(WIN_STEP):
        parted[k] = x_ref[k].astype(jnp.float32)
        real = parted[k, pl.ds(0, channels, stride=2), :]
        imag = parted[k, pl.ds(1, channels, stride=2), :]
        power = real * real + imag * imag
        high = power.astype(jnp.bfloat16)
        low = (power - high.astype(jnp.float32)).astype(jnp.bfloat16)
        sums = lax.dot_general(
            band[...], jnp.concatenate([high, low], 1), along, preferred_element_type=jnp.float32
        )
        both = jnp.concatenate([real.astype(jnp.bfloat16), imag.astype(jnp.bfloat16)], 1)
        picked = lax.dot_general(picker[...], both, along, preferred_element_type=jnp.float32)
        level = sums[kept:kept + 1] * (0.1 / FB) + 1e-06
        scale = lax.rsqrt(sums[:kept] * (1.0 / (2 * HALF_SPAN + 1)) + level)
        window = step * WIN_STEP + k
        gain = quality[pl.ds(window, 1), :] * scale
        local = lax.rem(window, WIN_GROUP)
        value = jnp.concatenate([picked[:kept] * gain, picked[kept:] * gain], 0)
        for c in range(0, channels, 128):
            staged[c // 128, pl.ds(local, 2 * kept, stride=WIN_GROUP), :] = value[:, c:c + 128]

    @pl.when(lax.rem(step, WIN_GROUP // WIN_STEP) == WIN_GROUP // WIN_STEP - 1)
    def _():
        for n in range(kept):
            share, place = n // (kept // shares), n % (kept // shares)
            for part in range(2):
                row = (part * kept + n) * WIN_GROUP
                for c in range(0, channels, 128):
                    value = staged[c // 128, row:row + WIN_GROUP, :].astype(jnp.bfloat16)
                    outs[place // depth][share, place % depth * 2 + part, :, c:c + 128] = value
        for share in range(shares):
            outs[-1][share, 2 * depth] = q_ref[pl.ds(group, WIN_GROUP), :]


def whiten(spectra, quality, bins, shares):
    windows, channels = quality.shape
    kept = bins.shape[0]
    paired = spectra.reshape(windows, channels * 2, FB)
    group = WIN_GROUP // WIN_STEP
    depth = kept // shares // PIECES
    rows = [2 * depth + (place == PIECES - 1) for place in range(PIECES)]
    return pl.pallas_call(
        lambda *refs: whiten_kernel(*refs, channels=channels, kept=kept, shares=shares, pieces=PIECES),
        grid=(windows // WIN_STEP,),
        in_specs=[
            pl.BlockSpec(memory_space=pltpu.SMEM),
            pl.BlockSpec((WIN_STEP, channels * 2, FB), lambda i: (i, 0, 0)),
            pl.BlockSpec((windows, channels), lambda i: (0, 0)),
        ],
        out_specs=[pl.BlockSpec((shares, r, WIN_GROUP, channels), lambda i: (0, 0, i // group, 0)) for r in rows],
        out_shape=[jax.ShapeDtypeStruct((shares, r, windows, channels), jnp.bfloat16) for r in rows],
        scratch_shapes=[
            pltpu.VMEM((WIN_STEP, channels * 2, FB), jnp.float32),
            pltpu.VMEM((kept + 16, 2 * FB), jnp.bfloat16),
            pltpu.VMEM((2 * kept, 2 * FB), jnp.bfloat16),
            pltpu.VMEM((channels // 128, 2 * kept * WIN_GROUP, 128), jnp.float32),
            pltpu.VMEM((windows, channels), jnp.float32),
        ],
        compiler_params=pltpu.CompilerParams(vmem_limit_bytes=60 * MIB),
        cost_estimate=taking(11),
    )(bins, paired, quality)


def turn_kernel(own_ref, out_ref):
    channels = own_ref.shape[-1]
    depth = out_ref.shape[-1]
    own = own_ref[...]
    out_ref[:channels] = own.reshape(depth, channels).T
    turned = jnp.concatenate([own[:, 1:], -own[:, :1]], 1)
    out_ref[channels:] = turned.reshape(depth, channels).T


def turn(own):
    shares, rows, windows, channels = own.shape
    deep = rows // 2
    depth = shares * 2 * windows
    return pl.pallas_call(
        turn_kernel,
        grid=(deep,),
        in_specs=[pl.BlockSpec((shares, 2, windows, channels), lambda n: (0, n, 0, 0))],
        out_specs=pl.BlockSpec((None, 2 * channels, depth), lambda n: (n, 0, 0)),
        out_shape=jax.ShapeDtypeStruct((deep, 2 * channels, depth), jnp.bfloat16),
        compiler_params=pltpu.CompilerParams(vmem_limit_bytes=63 * MIB),
        cost_estimate=taking(1.5),
    )(own)


def weight_kernel(where_ref, own_ref, first_ref, second_ref, both_ref, out_ref):
    shares, _, windows, channels = own_ref.shape
    depth = shares * windows
    own = own_ref[...].reshape(depth, channels).T
    for r, other in enumerate([jnp.where(where_ref[0] == 0, first_ref[...], second_ref[...]), both_ref[...]]):
        counts = jnp.dot(own, other.reshape(depth, channels), preferred_element_type=jnp.float32)
        out_ref[r] = lax.rsqrt(jnp.maximum(counts, 1.0))


def weights(where, *marks):
    channels = marks[0].shape[-1]
    return pl.pallas_call(
        weight_kernel,
        grid=(1,),
        in_specs=[pl.BlockSpec(memory_space=pltpu.SMEM)]
        + [pl.BlockSpec(value.shape, lambda g: (0, 0, 0, 0)) for value in marks],
        out_specs=pl.BlockSpec((2, channels, channels), lambda g: (0, 0, 0)),
        out_shape=jax.ShapeDtypeStruct((2, channels, channels), jnp.float32),
        compiler_params=pltpu.CompilerParams(vmem_limit_bytes=16 * MIB),
        cost_estimate=taking(1),
    )(where, *marks)


def cross_kernel(where_ref, weight_ref, *refs, jobs, deep, rounds):
    out_ref = refs[-1]
    channels = out_ref.shape[-1]
    depth = refs[jobs[0][0]].shape[-1]
    job, n = pl.program_id(0) // deep, lax.rem(pl.program_id(0), deep)
    rows = channels // CHUNKS

    def products(left_ref, other_ref, r):
        other = other_ref[...].reshape(depth, channels)
        for part in range(2):
            for i in range(CHUNKS):
                left = left_ref[n, part * channels + i * rows:part * channels + (i + 1) * rows]
                product = jnp.dot(left, other, preferred_element_type=jnp.float32)
                weight = weight_ref[r, i * rows:(i + 1) * rows]
                out_ref[part, i * rows:(i + 1) * rows] = (product * weight).astype(jnp.bfloat16)

    for at, (left, _, r, sources) in enumerate(jobs):
        for place, (source, core, last) in enumerate(sources):
            wanted = job == at
            if core is not None:
                wanted = wanted & (where_ref[0] == core)
            if last is not None:
                wanted = wanted & (where_ref[1] == last)

            @pl.when(wanted)
            def _(left=left, source=source, r=r):
                products(refs[left], refs[source], r - rounds[0])


def cross(where, weight, jobs, kept, held):
    arrays, plan, first_job = [], [], []

    def put(value, job):
        for at, other in enumerate(arrays):
            if other is value:
                return at
        arrays.append(value)
        first_job.append(job)
        return len(arrays) - 1

    lefts = []
    for at, (left, place, r, choices) in enumerate(jobs):
        lefts.append(put(left, None))
    for at, (left, place, r, choices) in enumerate(jobs):
        plan.append((lefts[at], place, r, [(put(value, at), core, last) for value, core, last in choices]))
    deep, double, depth = jobs[0][0].shape
    channels = double // 2
    extra = [] if held is None else [held]
    used = sorted({r for _, _, r, _ in plan})
    rounds = (used[0] // 2 * 2, 2) if len(used) > 1 else (used[0], 1)

    def spec(value, job):
        if job is None:
            return pl.BlockSpec(value.shape, lambda g: (0, 0, 0), pipeline_mode=pl.Buffered(1))
        shares, _, windows, _ = value.shape
        return pl.BlockSpec(
            (shares, 2, windows, channels), lambda g: (0, jnp.clip(g - job * deep, 0, deep - 1), 0, 0)
        )

    def chosen(job, values):
        result = values[0]
        for at in range(1, len(values)):
            result = jnp.where(job == at, values[at], result)
        return result

    def target(g):
        job = g // deep
        place = chosen(job, [p[1] for p in plan]) + lax.rem(g, deep)
        return chosen(job, [p[2] for p in plan]), 0, place, 0, 0

    return pl.pallas_call(
        lambda *refs: cross_kernel(*refs, jobs=plan, deep=deep, rounds=rounds),
        grid=(len(plan) * deep,),
        in_specs=[pl.BlockSpec(memory_space=pltpu.SMEM)]
        + [
            pl.BlockSpec(
                (rounds[1], channels, channels), lambda g: (rounds[0] % 2 // rounds[1], 0, 0), pipeline_mode=pl.Buffered(1)
            )
        ]
        + [spec(value, job) for value, job in zip(arrays, first_job)]
        + [pl.BlockSpec(memory_space=pl.ANY)] * len(extra),
        out_specs=pl.BlockSpec((None, 2, None, channels, channels), target),
        out_shape=jax.ShapeDtypeStruct((ROUNDS, 2, kept, channels, channels), jnp.bfloat16),
        input_output_aliases={} if held is None else {2 + len(arrays): 0},
        compiler_params=pltpu.CompilerParams(vmem_limit_bytes=32 * MIB),
        cost_estimate=taking(1),
    )(where, weight, *arrays, *extra)


def tied(*values):
    return lax.optimization_barrier(values)


def gate_kernel(value_ref, *refs):
    del value_ref, refs


def gated(value, *others):
    anywhere = pl.BlockSpec(memory_space=pl.ANY)
    return pl.pallas_call(
        gate_kernel,
        in_specs=[anywhere] * (1 + len(others)),
        out_specs=anywhere,
        out_shape=jax.ShapeDtypeStruct(value.shape, value.dtype),
        input_output_aliases={0: 0},
        cost_estimate=taking(0.1),
    )(value, *others)


def shards(spectra, quality, bins):
    blocks = lax.axis_size("blk")
    shares = lax.axis_size("bin")
    chips = blocks // 2
    block = lax.axis_index("blk")
    where = jnp.stack([block % 2, (block // 2 % ROWS_Z == ROWS_Z - 1).astype(jnp.int32)])

    def moved(value, pairs):
        return lax.ppermute(value, "blk", [(2 * s + c, 2 * t + c) for s, t in pairs for c in range(2)])

    def back(value):
        return moved(value, [((t + 1) % chips, t) for t in range(chips)])

    def chip(row, z):
        return (row % (chips // ROWS_Z)) * ROWS_Z + z % ROWS_Z

    every = [(row, z) for row in range(chips // ROWS_Z) for z in range(ROWS_Z)]

    def forth(value):
        return moved(value, [(chip(row, z - 1), chip(row, z)) for row, z in every])

    def forth_last(value):
        return moved(value, [(chip(row + (z + 2) // ROWS_Z, z - 1), chip(row, z)) for row, z in every])

    def swapped(value):
        return lax.ppermute(value, "blk", [(i, i ^ 1) for i in range(blocks)])

    def back_inside(value):
        return moved(value, [(chip(row, z + 1), chip(row, z)) for row, z in every])

    def last_crossed(value):
        rows = chips // ROWS_Z
        return moved(value, [(chip(row + 1, -1), chip(row, -1)) for row in range(rows)])

    def far_back(value):
        return moved(value, [((t + 2) % chips, t) for t in range(chips)])

    def to_bins(value):
        return lax.all_to_all(value, "bin", split_axis=0, concat_axis=0, tiled=True)

    kept = bins.shape[0] // shares
    deep = kept // PIECES
    sent_a, sent_b = whiten(spectra, quality, bins, shares)
    own_a = to_bins(sent_a)
    sent_b, own_a = tied(sent_b, own_a)
    own_all = to_bins(sent_b)
    own_b, own_marks = own_all[:, :2 * deep], own_all[:, 2 * deep:]
    inside_a, forth_a, forth_marks = back_inside(own_a), forth(own_a), forth(own_marks)
    left_a = turn(own_a)
    own_b, inside_a, forth_a, forth_marks, left_a = tied(own_b, inside_a, forth_a, forth_marks, left_a)
    near_b, crossed_a, far_a = back(own_b), last_crossed(inside_a), forth_last(forth_a)
    near_marks, far_marks = back(own_marks), forth_last(forth_marks)
    left_b = turn(own_b)
    near_b, crossed_a, far_a, left_b = tied(near_b, crossed_a, far_a, left_b)
    far_b = back(near_b)
    near_marks_pair = swapped(near_marks)
    own_pair_a, own_pair_b, inside_pair_a = swapped(own_a), swapped(own_b), swapped(inside_a)
    own_marks_pair, far_marks_pair = swapped(own_marks), swapped(far_marks)
    crossed_pair_a, near_pair_b, far_pair_a = swapped(crossed_a), swapped(near_b), swapped(far_a)
    weight = weights(where, own_marks, own_marks_pair, near_marks_pair, near_marks)
    far_weight = weights(where, own_marks, near_marks_pair, far_marks_pair, far_marks)
    jobs = [
        (left_b, deep, 1, [(near_b, None, None)]),
        (left_b, deep, 0, [(own_pair_b, 0, None), (near_pair_b, 1, None)]),
        (left_a, 0, 1, [(inside_a, None, 0), (crossed_a, None, 1)]),
        (left_a, 0, 0, [(own_pair_a, 0, None), (inside_pair_a, 1, 0), (crossed_pair_a, 1, 1)]),
    ]
    out = cross(where, weight, jobs, kept, None)
    jobs = [
        (left_a, 0, 3, [(far_a, None, None)]),
        (left_a, 0, 2, [(inside_pair_a, 0, 0), (crossed_pair_a, 0, 1), (far_pair_a, 1, None)]),
    ]
    out = cross(where, far_weight, jobs, kept, out)
    far_b, out = tied(far_b, out)
    far_pair_b = swapped(far_b)
    out = cross(where, far_weight, [(left_b, deep, 3, [(far_b, None, None)])], kept, out)
    return cross(where, far_weight, [(left_b, deep, 2, [(near_pair_b, 0, None), (far_pair_b, 1, None)])], kept, out)


def solution(mesh):
    return jax.shard_map(
        shards,
        mesh=mesh,
        in_specs=(P("bin", "blk", None, None), P("bin", "blk"), P()),
        out_specs=P(None, None, "bin", "blk", None),
        check_vma=False,
    )
```

```python
import jax
import jax.numpy as jnp
from jax import lax
from jax.experimental import pallas as pl
from jax.experimental.pallas import tpu as pltpu
from jax.sharding import PartitionSpec as P

FB = 128
HALF_SPAN = 4
ROUNDS = 4
ROWS_Z = 4
WIN_STEP = 8
WIN_GROUP = 16
PIECES = 2
CHUNKS = 2
MIB = 1024 * 1024
COST = 1000


def taking(micros):
    return pl.CostEstimate(flops=int(micros * COST), bytes_accessed=1000, transcendentals=0)


def whiten_kernel(bins_ref, x_ref, q_ref, *refs, channels, kept, shares, pieces):
    outs = refs[:pieces]
    parted, band, picker, staged, quality = refs[pieces:]
    depth = kept // shares // pieces
    step = pl.program_id(0)
    group = pl.multiple_of(step * WIN_STEP // WIN_GROUP * WIN_GROUP, WIN_GROUP)

    @pl.when(step == 0)
    def _():
        quality[...] = q_ref[...].astype(jnp.float32)
        lanes = lax.broadcasted_iota(jnp.int32, (kept, 2 * FB), 1)
        rows = lax.broadcasted_iota(jnp.int32, (kept, 2 * FB), 0)
        wanted = jnp.zeros((kept, 2 * FB), jnp.int32)
        for n in range(kept):
            wanted = jnp.where(rows == n, bins_ref[n], wanted)
        offset = jnp.where(lanes >= FB, lanes - FB, lanes)
        near = jnp.abs(offset - wanted) <= HALF_SPAN
        band[:kept] = jnp.where(near, 1.0, 0.0).astype(jnp.bfloat16)
        band[kept:] = jnp.ones((16, 2 * FB), jnp.bfloat16)
        exact = offset == wanted
        picker[:kept] = jnp.where(exact & (lanes < FB), 1.0, 0.0).astype(jnp.bfloat16)
        picker[kept:] = jnp.where(exact & (lanes >= FB), 1.0, 0.0).astype(jnp.bfloat16)

    along = (((1,), (1,)), ((), ()))
    for k in range(WIN_STEP):
        parted[k] = x_ref[k].astype(jnp.float32)
        real = parted[k, pl.ds(0, channels, stride=2), :]
        imag = parted[k, pl.ds(1, channels, stride=2), :]
        power = real * real + imag * imag
        high = power.astype(jnp.bfloat16)
        low = (power - high.astype(jnp.float32)).astype(jnp.bfloat16)
        sums = lax.dot_general(
            band[...], jnp.concatenate([high, low], 1), along, preferred_element_type=jnp.float32
        )
        both = jnp.concatenate([real.astype(jnp.bfloat16), imag.astype(jnp.bfloat16)], 1)
        picked = lax.dot_general(picker[...], both, along, preferred_element_type=jnp.float32)
        level = sums[kept:kept + 1] * (0.1 / FB) + 1e-06
        scale = lax.rsqrt(sums[:kept] * (1.0 / (2 * HALF_SPAN + 1)) + level)
        window = step * WIN_STEP + k
        gain = quality[pl.ds(window, 1), :] * scale
        local = lax.rem(window, WIN_GROUP)
        value = jnp.concatenate([picked[:kept] * gain, picked[kept:] * gain], 0)
        for c in range(0, channels, 128):
            staged[c // 128, pl.ds(local, 2 * kept, stride=WIN_GROUP), :] = value[:, c:c + 128]

    @pl.when(lax.rem(step, WIN_GROUP // WIN_STEP) == WIN_GROUP // WIN_STEP - 1)
    def _():
        for n in range(kept):
            share, place = n // (kept // shares), n % (kept // shares)
            for part in range(2):
                row = (part * kept + n) * WIN_GROUP
                for c in range(0, channels, 128):
                    value = staged[c // 128, row:row + WIN_GROUP, :].astype(jnp.bfloat16)
                    outs[place // depth][share, place % depth * 2 + part, :, c:c + 128] = value
        for share in range(shares):
            outs[-1][share, 2 * depth] = q_ref[pl.ds(group, WIN_GROUP), :]


def whiten(spectra, quality, bins, shares):
    windows, channels = quality.shape
    kept = bins.shape[0]
    paired = spectra.reshape(windows, channels * 2, FB)
    group = WIN_GROUP // WIN_STEP
    depth = kept // shares // PIECES
    rows = [2 * depth + (place == PIECES - 1) for place in range(PIECES)]
    return pl.pallas_call(
        lambda *refs: whiten_kernel(*refs, channels=channels, kept=kept, shares=shares, pieces=PIECES),
        grid=(windows // WIN_STEP,),
        in_specs=[
            pl.BlockSpec(memory_space=pltpu.SMEM),
            pl.BlockSpec((WIN_STEP, channels * 2, FB), lambda i: (i, 0, 0)),
            pl.BlockSpec((windows, channels), lambda i: (0, 0)),
        ],
        out_specs=[pl.BlockSpec((shares, r, WIN_GROUP, channels), lambda i: (0, 0, i // group, 0)) for r in rows],
        out_shape=[jax.ShapeDtypeStruct((shares, r, windows, channels), jnp.bfloat16) for r in rows],
        scratch_shapes=[
            pltpu.VMEM((WIN_STEP, channels * 2, FB), jnp.float32),
            pltpu.VMEM((kept + 16, 2 * FB), jnp.bfloat16),
            pltpu.VMEM((2 * kept, 2 * FB), jnp.bfloat16),
            pltpu.VMEM((channels // 128, 2 * kept * WIN_GROUP, 128), jnp.float32),
            pltpu.VMEM((windows, channels), jnp.float32),
        ],
        compiler_params=pltpu.CompilerParams(vmem_limit_bytes=60 * MIB),
        cost_estimate=taking(11),
    )(bins, paired, quality)


def turn_kernel(own_ref, out_ref):
    channels = own_ref.shape[-1]
    depth = out_ref.shape[-1]
    own = own_ref[...]
    out_ref[:channels] = own.reshape(depth, channels).T
    turned = jnp.concatenate([own[:, 1:], -own[:, :1]], 1)
    out_ref[channels:] = turned.reshape(depth, channels).T


def turn(own):
    shares, rows, windows, channels = own.shape
    deep = rows // 2
    depth = shares * 2 * windows
    return pl.pallas_call(
        turn_kernel,
        grid=(deep,),
        in_specs=[pl.BlockSpec((shares, 2, windows, channels), lambda n: (0, n, 0, 0))],
        out_specs=pl.BlockSpec((None, 2 * channels, depth), lambda n: (n, 0, 0)),
        out_shape=jax.ShapeDtypeStruct((deep, 2 * channels, depth), jnp.bfloat16),
        compiler_params=pltpu.CompilerParams(vmem_limit_bytes=63 * MIB),
        cost_estimate=taking(1.5),
    )(own)


def weight_kernel(where_ref, own_ref, first_ref, second_ref, both_ref, out_ref):
    shares, _, windows, channels = own_ref.shape
    depth = shares * windows
    own = own_ref[...].reshape(depth, channels).T
    for r, other in enumerate([jnp.where(where_ref[0] == 0, first_ref[...], second_ref[...]), both_ref[...]]):
        counts = jnp.dot(own, other.reshape(depth, channels), preferred_element_type=jnp.float32)
        out_ref[r] = lax.rsqrt(jnp.maximum(counts, 1.0))


def weights(where, *marks):
    channels = marks[0].shape[-1]
    return pl.pallas_call(
        weight_kernel,
        grid=(1,),
        in_specs=[pl.BlockSpec(memory_space=pltpu.SMEM)]
        + [pl.BlockSpec(value.shape, lambda g: (0, 0, 0, 0)) for value in marks],
        out_specs=pl.BlockSpec((2, channels, channels), lambda g: (0, 0, 0)),
        out_shape=jax.ShapeDtypeStruct((2, channels, channels), jnp.float32),
        compiler_params=pltpu.CompilerParams(vmem_limit_bytes=16 * MIB),
        cost_estimate=taking(1),
    )(where, *marks)


def cross_kernel(where_ref, weight_ref, *refs, jobs, deep, rounds):
    out_ref = refs[-1]
    channels = out_ref.shape[-1]
    depth = refs[jobs[0][0]].shape[-1]
    job, n = pl.program_id(0) // deep, lax.rem(pl.program_id(0), deep)
    rows = channels // CHUNKS

    def products(left_ref, other_ref, r):
        other = other_ref[...].reshape(depth, channels)
        for part in range(2):
            for i in range(CHUNKS):
                left = left_ref[n, part * channels + i * rows:part * channels + (i + 1) * rows]
                product = jnp.dot(left, other, preferred_element_type=jnp.float32)
                weight = weight_ref[r, i * rows:(i + 1) * rows]
                out_ref[part, i * rows:(i + 1) * rows] = (product * weight).astype(jnp.bfloat16)

    for at, (left, _, r, sources) in enumerate(jobs):
        for place, (source, core, last) in enumerate(sources):
            wanted = job == at
            if core is not None:
                wanted = wanted & (where_ref[0] == core)
            if last is not None:
                wanted = wanted & (where_ref[1] == last)

            @pl.when(wanted)
            def _(left=left, source=source, r=r):
                products(refs[left], refs[source], r - rounds[0])


def cross(where, weight, jobs, kept, held):
    arrays, plan, first_job = [], [], []

    def put(value, job):
        for at, other in enumerate(arrays):
            if other is value:
                return at
        arrays.append(value)
        first_job.append(job)
        return len(arrays) - 1

    lefts = []
    for at, (left, place, r, choices) in enumerate(jobs):
        lefts.append(put(left, None))
    for at, (left, place, r, choices) in enumerate(jobs):
        plan.append((lefts[at], place, r, [(put(value, at), core, last) for value, core, last in choices]))
    deep, double, depth = jobs[0][0].shape
    channels = double // 2
    extra = [] if held is None else [held]
    used = sorted({r for _, _, r, _ in plan})
    rounds = (used[0] // 2 * 2, 2) if len(used) > 1 else (used[0], 1)

    def spec(value, job):
        if job is None:
            return pl.BlockSpec(value.shape, lambda g: (0, 0, 0), pipeline_mode=pl.Buffered(1))
        shares, _, windows, _ = value.shape
        return pl.BlockSpec(
            (shares, 2, windows, channels), lambda g: (0, jnp.clip(g - job * deep, 0, deep - 1), 0, 0)
        )

    def chosen(job, values):
        result = values[0]
        for at in range(1, len(values)):
            result = jnp.where(job == at, values[at], result)
        return result

    def target(g):
        job = g // deep
        place = chosen(job, [p[1] for p in plan]) + lax.rem(g, deep)
        return chosen(job, [p[2] for p in plan]), 0, place, 0, 0

    return pl.pallas_call(
        lambda *refs: cross_kernel(*refs, jobs=plan, deep=deep, rounds=rounds),
        grid=(len(plan) * deep,),
        in_specs=[pl.BlockSpec(memory_space=pltpu.SMEM)]
        + [
            pl.BlockSpec(
                (rounds[1], channels, channels), lambda g: (rounds[0] % 2 // rounds[1], 0, 0), pipeline_mode=pl.Buffered(1)
            )
        ]
        + [spec(value, job) for value, job in zip(arrays, first_job)]
        + [pl.BlockSpec(memory_space=pl.ANY)] * len(extra),
        out_specs=pl.BlockSpec((None, 2, None, channels, channels), target),
        out_shape=jax.ShapeDtypeStruct((ROUNDS, 2, kept, channels, channels), jnp.bfloat16),
        input_output_aliases={} if held is None else {2 + len(arrays): 0},
        compiler_params=pltpu.CompilerParams(vmem_limit_bytes=32 * MIB),
        cost_estimate=taking(1),
    )(where, weight, *arrays, *extra)


def copied_kernel(value_ref, out_ref):
    for at in range(value_ref.shape[0]):
        out_ref[at] = value_ref[at]


def copied(value):
    scalars = pl.BlockSpec(memory_space=pltpu.SMEM)
    return pl.pallas_call(
        copied_kernel,
        in_specs=[scalars],
        out_specs=scalars,
        out_shape=jax.ShapeDtypeStruct(value.shape, value.dtype),
        compiler_params=pltpu.CompilerParams(vmem_limit_bytes=63 * MIB),
        cost_estimate=taking(0.1),
    )(value)


def tied(*values):
    return lax.optimization_barrier(values)


def gate_kernel(value_ref, *refs):
    del value_ref, refs


def gated(value, *others):
    anywhere = pl.BlockSpec(memory_space=pl.ANY)
    return pl.pallas_call(
        gate_kernel,
        in_specs=[anywhere] * (1 + len(others)),
        out_specs=anywhere,
        out_shape=jax.ShapeDtypeStruct(value.shape, value.dtype),
        input_output_aliases={0: 0},
        cost_estimate=taking(0.1),
    )(value, *others)


def shards(spectra, quality, bins):
    blocks = lax.axis_size("blk")
    shares = lax.axis_size("bin")
    chips = blocks // 2
    block = lax.axis_index("blk")
    where = jnp.stack([block % 2, (block // 2 % ROWS_Z == ROWS_Z - 1).astype(jnp.int32)])

    def moved(value, pairs):
        return lax.ppermute(value, "blk", [(2 * s + c, 2 * t + c) for s, t in pairs for c in range(2)])

    def back(value):
        return moved(value, [((t + 1) % chips, t) for t in range(chips)])

    def chip(row, z):
        return (row % (chips // ROWS_Z)) * ROWS_Z + z % ROWS_Z

    every = [(row, z) for row in range(chips // ROWS_Z) for z in range(ROWS_Z)]

    def forth(value):
        return moved(value, [(chip(row, z - 1), chip(row, z)) for row, z in every])

    def forth_last(value):
        return moved(value, [(chip(row + (z + 2) // ROWS_Z, z - 1), chip(row, z)) for row, z in every])

    def swapped(value):
        return lax.ppermute(value, "blk", [(i, i ^ 1) for i in range(blocks)])

    def back_inside(value):
        return moved(value, [(chip(row, z + 1), chip(row, z)) for row, z in every])

    def last_crossed(value):
        rows = chips // ROWS_Z
        return moved(value, [(chip(row + 1, -1), chip(row, -1)) for row in range(rows)])

    def far_back(value):
        return moved(value, [((t + 2) % chips, t) for t in range(chips)])

    def to_bins(value):
        return lax.all_to_all(value, "bin", split_axis=0, concat_axis=0, tiled=True)

    kept = bins.shape[0] // shares
    deep = kept // PIECES
    sent_a, sent_b = whiten(spectra, quality, bins, shares)
    own_a = to_bins(sent_a)
    sent_b, own_a = tied(sent_b, own_a)
    own_all = to_bins(sent_b)
    own_b, own_marks = own_all[:, :2 * deep], own_all[:, 2 * deep:]
    inside_a, forth_a, forth_marks = back_inside(own_a), forth(own_a), forth(own_marks)
    left_a = turn(own_a)
    own_b, inside_a, forth_a, forth_marks, left_a = tied(own_b, inside_a, forth_a, forth_marks, left_a)
    near_b, crossed_a, far_a = back(own_b), last_crossed(inside_a), forth_last(forth_a)
    left_b = turn(own_b)
    forth_marks, left_b = tied(forth_marks, left_b)
    near_marks, far_marks = back(own_marks), forth_last(forth_marks)
    near_b, crossed_a, far_a, where = tied(near_b, crossed_a, far_a, copied(where))
    far_b = back(near_b)
    near_marks_pair = swapped(near_marks)
    own_pair_a, own_pair_b, inside_pair_a = swapped(own_a), swapped(own_b), swapped(inside_a)
    own_marks_pair, far_marks_pair = swapped(own_marks), swapped(far_marks)
    crossed_pair_a, near_pair_b, far_pair_a = swapped(crossed_a), swapped(near_b), swapped(far_a)
    weight = weights(where, own_marks, own_marks_pair, near_marks_pair, near_marks)
    far_weight = weights(where, own_marks, near_marks_pair, far_marks_pair, far_marks)
    jobs = [
        (left_b, deep, 1, [(near_b, None, None)]),
        (left_b, deep, 0, [(own_pair_b, 0, None), (near_pair_b, 1, None)]),
        (left_a, 0, 1, [(inside_a, None, 0), (crossed_a, None, 1)]),
        (left_a, 0, 0, [(own_pair_a, 0, None), (inside_pair_a, 1, 0), (crossed_pair_a, 1, 1)]),
    ]
    out = cross(where, weight, jobs, kept, None)
    jobs = [
        (left_a, 0, 3, [(far_a, None, None)]),
        (left_a, 0, 2, [(inside_pair_a, 0, 0), (crossed_pair_a, 0, 1), (far_pair_a, 1, None)]),
    ]
    out = cross(where, far_weight, jobs, kept, out)
    far_b, out = tied(far_b, out)
    far_pair_b = swapped(far_b)
    out = cross(where, far_weight, [(left_b, deep, 3, [(far_b, None, None)])], kept, out)
    return cross(where, far_weight, [(left_b, deep, 2, [(near_pair_b, 0, None), (far_pair_b, 1, None)])], kept, out)


def solution(mesh):
    return jax.shard_map(
        shards,
        mesh=mesh,
        in_specs=(P("bin", "blk", None, None), P("bin", "blk"), P()),
        out_specs=P(None, None, "bin", "blk", None),
        check_vma=False,
    )
```

```python
import jax
import jax.numpy as jnp
from jax import lax
from jax.experimental import pallas as pl
from jax.experimental.pallas import tpu as pltpu
from jax.sharding import PartitionSpec as P

FB = 128
HALF_SPAN = 4
ROUNDS = 4
ROWS_Z = 4
WIN_STEP = 8
WIN_GROUP = 16
PIECES = 2
CHUNKS = 2
MIB = 1024 * 1024
COST = 1000


def taking(micros):
    return pl.CostEstimate(flops=int(micros * COST), bytes_accessed=1000, transcendentals=0)


def whiten_kernel(bins_ref, x_ref, q_ref, *refs, channels, kept, shares, pieces):
    outs = refs[:pieces]
    parted, band, picker, staged, quality = refs[pieces:]
    depth = kept // shares // pieces
    step = pl.program_id(0)
    group = pl.multiple_of(step * WIN_STEP // WIN_GROUP * WIN_GROUP, WIN_GROUP)

    @pl.when(step == 0)
    def _():
        quality[...] = q_ref[...].astype(jnp.float32)
        lanes = lax.broadcasted_iota(jnp.int32, (kept, 2 * FB), 1)
        rows = lax.broadcasted_iota(jnp.int32, (kept, 2 * FB), 0)
        wanted = jnp.zeros((kept, 2 * FB), jnp.int32)
        for n in range(kept):
            wanted = jnp.where(rows == n, bins_ref[n], wanted)
        offset = jnp.where(lanes >= FB, lanes - FB, lanes)
        near = jnp.abs(offset - wanted) <= HALF_SPAN
        band[:kept] = jnp.where(near, 1.0, 0.0).astype(jnp.bfloat16)
        band[kept:] = jnp.ones((16, 2 * FB), jnp.bfloat16)
        exact = offset == wanted
        picker[:kept] = jnp.where(exact & (lanes < FB), 1.0, 0.0).astype(jnp.bfloat16)
        picker[kept:] = jnp.where(exact & (lanes >= FB), 1.0, 0.0).astype(jnp.bfloat16)

    along = (((1,), (1,)), ((), ()))
    for k in range(WIN_STEP):
        parted[k] = x_ref[k].astype(jnp.float32)
        real = parted[k, pl.ds(0, channels, stride=2), :]
        imag = parted[k, pl.ds(1, channels, stride=2), :]
        power = real * real + imag * imag
        high = power.astype(jnp.bfloat16)
        low = (power - high.astype(jnp.float32)).astype(jnp.bfloat16)
        sums = lax.dot_general(
            band[...], jnp.concatenate([high, low], 1), along, preferred_element_type=jnp.float32
        )
        both = jnp.concatenate([real.astype(jnp.bfloat16), imag.astype(jnp.bfloat16)], 1)
        picked = lax.dot_general(picker[...], both, along, preferred_element_type=jnp.float32)
        level = sums[kept:kept + 1] * (0.1 / FB) + 1e-06
        scale = lax.rsqrt(sums[:kept] * (1.0 / (2 * HALF_SPAN + 1)) + level)
        window = step * WIN_STEP + k
        gain = quality[pl.ds(window, 1), :] * scale
        local = lax.rem(window, WIN_GROUP)
        value = jnp.concatenate([picked[:kept] * gain, picked[kept:] * gain], 0)
        for c in range(0, channels, 128):
            staged[c // 128, pl.ds(local, 2 * kept, stride=WIN_GROUP), :] = value[:, c:c + 128]

    @pl.when(lax.rem(step, WIN_GROUP // WIN_STEP) == WIN_GROUP // WIN_STEP - 1)
    def _():
        for n in range(kept):
            share, place = n // (kept // shares), n % (kept // shares)
            for part in range(2):
                row = (part * kept + n) * WIN_GROUP
                for c in range(0, channels, 128):
                    value = staged[c // 128, row:row + WIN_GROUP, :].astype(jnp.bfloat16)
                    outs[place // depth][share, place % depth * 2 + part, :, c:c + 128] = value
        for share in range(shares):
            outs[-1][share, 2 * depth] = q_ref[pl.ds(group, WIN_GROUP), :]


def whiten(spectra, quality, bins, shares):
    windows, channels = quality.shape
    kept = bins.shape[0]
    paired = spectra.reshape(windows, channels * 2, FB)
    group = WIN_GROUP // WIN_STEP
    depth = kept // shares // PIECES
    rows = [2 * depth + (place == PIECES - 1) for place in range(PIECES)]
    return pl.pallas_call(
        lambda *refs: whiten_kernel(*refs, channels=channels, kept=kept, shares=shares, pieces=PIECES),
        grid=(windows // WIN_STEP,),
        in_specs=[
            pl.BlockSpec(memory_space=pltpu.SMEM),
            pl.BlockSpec((WIN_STEP, channels * 2, FB), lambda i: (i, 0, 0)),
            pl.BlockSpec((windows, channels), lambda i: (0, 0)),
        ],
        out_specs=[pl.BlockSpec((shares, r, WIN_GROUP, channels), lambda i: (0, 0, i // group, 0)) for r in rows],
        out_shape=[jax.ShapeDtypeStruct((shares, r, windows, channels), jnp.bfloat16) for r in rows],
        scratch_shapes=[
            pltpu.VMEM((WIN_STEP, channels * 2, FB), jnp.float32),
            pltpu.VMEM((kept + 16, 2 * FB), jnp.bfloat16),
            pltpu.VMEM((2 * kept, 2 * FB), jnp.bfloat16),
            pltpu.VMEM((channels // 128, 2 * kept * WIN_GROUP, 128), jnp.float32),
            pltpu.VMEM((windows, channels), jnp.float32),
        ],
        compiler_params=pltpu.CompilerParams(vmem_limit_bytes=60 * MIB),
        cost_estimate=taking(11),
    )(bins, paired, quality)


def turn_kernel(own_ref, out_ref):
    channels = own_ref.shape[-1]
    depth = out_ref.shape[-1]
    own = own_ref[...]
    out_ref[:channels] = own.reshape(depth, channels).T
    turned = jnp.concatenate([own[:, 1:], -own[:, :1]], 1)
    out_ref[channels:] = turned.reshape(depth, channels).T


def turn(own):
    shares, rows, windows, channels = own.shape
    deep = rows // 2
    depth = shares * 2 * windows
    return pl.pallas_call(
        turn_kernel,
        grid=(deep,),
        in_specs=[pl.BlockSpec((shares, 2, windows, channels), lambda n: (0, n, 0, 0))],
        out_specs=pl.BlockSpec((None, 2 * channels, depth), lambda n: (n, 0, 0)),
        out_shape=jax.ShapeDtypeStruct((deep, 2 * channels, depth), jnp.bfloat16),
        compiler_params=pltpu.CompilerParams(vmem_limit_bytes=63 * MIB),
        cost_estimate=taking(1.5),
    )(own)


def weight_kernel(where_ref, own_ref, first_ref, second_ref, both_ref, out_ref):
    shares, _, windows, channels = own_ref.shape
    depth = shares * windows
    own = own_ref[...].reshape(depth, channels).T
    for r, other in enumerate([jnp.where(where_ref[0] == 0, first_ref[...], second_ref[...]), both_ref[...]]):
        counts = jnp.dot(own, other.reshape(depth, channels), preferred_element_type=jnp.float32)
        out_ref[r] = lax.rsqrt(jnp.maximum(counts, 1.0))


def weights(where, *marks):
    channels = marks[0].shape[-1]
    return pl.pallas_call(
        weight_kernel,
        grid=(1,),
        in_specs=[pl.BlockSpec(memory_space=pltpu.SMEM)]
        + [pl.BlockSpec(value.shape, lambda g: (0, 0, 0, 0)) for value in marks],
        out_specs=pl.BlockSpec((2, channels, channels), lambda g: (0, 0, 0)),
        out_shape=jax.ShapeDtypeStruct((2, channels, channels), jnp.float32),
        compiler_params=pltpu.CompilerParams(vmem_limit_bytes=16 * MIB),
        cost_estimate=taking(1),
    )(where, *marks)


def cross_kernel(where_ref, weight_ref, *refs, jobs, deep, rounds):
    out_ref = refs[-1]
    channels = out_ref.shape[-1]
    depth = refs[jobs[0][0]].shape[-1]
    job, n = pl.program_id(0) // deep, lax.rem(pl.program_id(0), deep)
    rows = channels // CHUNKS

    def products(left_ref, other_ref, r):
        other = other_ref[...].reshape(depth, channels)
        for part in range(2):
            for i in range(CHUNKS):
                left = left_ref[n if left_ref.shape[0] > 1 else 0, part * channels + i * rows:part * channels + (i + 1) * rows]
                product = jnp.dot(left, other, preferred_element_type=jnp.float32)
                weight = weight_ref[r, i * rows:(i + 1) * rows]
                out_ref[part, i * rows:(i + 1) * rows] = (product * weight).astype(jnp.bfloat16)

    for at, (left, _, r, sources) in enumerate(jobs):
        for place, (source, core, last) in enumerate(sources):
            wanted = job == at
            if core is not None:
                wanted = wanted & (where_ref[0] == core)
            if last is not None:
                wanted = wanted & (where_ref[1] == last)

            @pl.when(wanted)
            def _(left=left, source=source, r=r):
                products(refs[left], refs[source], r - rounds[0])


def cross(where, weight, jobs, kept, held):
    arrays, plan, first_job = [], [], []

    def put(value, job):
        for at, other in enumerate(arrays):
            if other is value:
                return at
        arrays.append(value)
        first_job.append(job)
        return len(arrays) - 1

    lefts = []
    for at, (left, place, r, choices) in enumerate(jobs):
        lefts.append(put(left, None))
    for at, (left, place, r, choices) in enumerate(jobs):
        plan.append((lefts[at], place, r, [(put(value, at), core, last) for value, core, last in choices]))
    deep, double, depth = jobs[0][0].shape
    channels = double // 2
    extra = [] if held is None else [held]
    used = sorted({r for _, _, r, _ in plan})
    rounds = (used[0] // 2 * 2, 2) if len(used) > 1 else (used[0], 1)

    def spec(value, job):
        if job is None:
            if len(plan) == 1:
                return pl.BlockSpec((1, double, depth), lambda g: (g, 0, 0))
            return pl.BlockSpec(value.shape, lambda g: (0, 0, 0), pipeline_mode=pl.Buffered(1))
        shares, _, windows, _ = value.shape
        return pl.BlockSpec(
            (shares, 2, windows, channels), lambda g: (0, jnp.clip(g - job * deep, 0, deep - 1), 0, 0)
        )

    def chosen(job, values):
        result = values[0]
        for at in range(1, len(values)):
            result = jnp.where(job == at, values[at], result)
        return result

    def target(g):
        job = g // deep
        place = chosen(job, [p[1] for p in plan]) + lax.rem(g, deep)
        return chosen(job, [p[2] for p in plan]), 0, place, 0, 0

    return pl.pallas_call(
        lambda *refs: cross_kernel(*refs, jobs=plan, deep=deep, rounds=rounds),
        grid=(len(plan) * deep,),
        in_specs=[pl.BlockSpec(memory_space=pltpu.SMEM)]
        + [
            pl.BlockSpec(
                (rounds[1], channels, channels), lambda g: (rounds[0] % 2 // rounds[1], 0, 0), pipeline_mode=pl.Buffered(1)
            )
        ]
        + [spec(value, job) for value, job in zip(arrays, first_job)]
        + [pl.BlockSpec(memory_space=pl.ANY)] * len(extra),
        out_specs=pl.BlockSpec((None, 2, None, channels, channels), target),
        out_shape=jax.ShapeDtypeStruct((ROUNDS, 2, kept, channels, channels), jnp.bfloat16),
        input_output_aliases={} if held is None else {2 + len(arrays): 0},
        compiler_params=pltpu.CompilerParams(vmem_limit_bytes=32 * MIB),
        cost_estimate=taking(1),
    )(where, weight, *arrays, *extra)


def copied_kernel(value_ref, out_ref):
    for at in range(value_ref.shape[0]):
        out_ref[at] = value_ref[at]


def copied(value):
    scalars = pl.BlockSpec(memory_space=pltpu.SMEM)
    return pl.pallas_call(
        copied_kernel,
        in_specs=[scalars],
        out_specs=scalars,
        out_shape=jax.ShapeDtypeStruct(value.shape, value.dtype),
        compiler_params=pltpu.CompilerParams(vmem_limit_bytes=63 * MIB),
        cost_estimate=taking(0.1),
    )(value)


def tied(*values):
    return lax.optimization_barrier(values)


def gate_kernel(value_ref, *refs):
    del value_ref, refs


def gated(value, *others):
    anywhere = pl.BlockSpec(memory_space=pl.ANY)
    return pl.pallas_call(
        gate_kernel,
        in_specs=[anywhere] * (1 + len(others)),
        out_specs=anywhere,
        out_shape=jax.ShapeDtypeStruct(value.shape, value.dtype),
        input_output_aliases={0: 0},
        cost_estimate=taking(0.1),
    )(value, *others)


def shards(spectra, quality, bins):
    blocks = lax.axis_size("blk")
    shares = lax.axis_size("bin")
    chips = blocks // 2
    block = lax.axis_index("blk")
    where = jnp.stack([block % 2, (block // 2 % ROWS_Z == ROWS_Z - 1).astype(jnp.int32)])

    def moved(value, pairs):
        return lax.ppermute(value, "blk", [(2 * s + c, 2 * t + c) for s, t in pairs for c in range(2)])

    def back(value):
        return moved(value, [((t + 1) % chips, t) for t in range(chips)])

    def chip(row, z):
        return (row % (chips // ROWS_Z)) * ROWS_Z + z % ROWS_Z

    every = [(row, z) for row in range(chips // ROWS_Z) for z in range(ROWS_Z)]

    def forth(value):
        return moved(value, [(chip(row, z - 1), chip(row, z)) for row, z in every])

    def forth_last(value):
        return moved(value, [(chip(row + (z + 2) // ROWS_Z, z - 1), chip(row, z)) for row, z in every])

    def swapped(value):
        return lax.ppermute(value, "blk", [(i, i ^ 1) for i in range(blocks)])

    def back_inside(value):
        return moved(value, [(chip(row, z + 1), chip(row, z)) for row, z in every])

    def last_crossed(value):
        rows = chips // ROWS_Z
        return moved(value, [(chip(row + 1, -1), chip(row, -1)) for row in range(rows)])

    def far_back(value):
        return moved(value, [((t + 2) % chips, t) for t in range(chips)])

    def to_bins(value):
        return lax.all_to_all(value, "bin", split_axis=0, concat_axis=0, tiled=True)

    kept = bins.shape[0] // shares
    deep = kept // PIECES
    sent_a, sent_b = whiten(spectra, quality, bins, shares)
    own_a = to_bins(sent_a)
    sent_b, own_a = tied(sent_b, own_a)
    own_all = to_bins(sent_b)
    own_b, own_marks = own_all[:, :2 * deep], own_all[:, 2 * deep:]
    inside_a, forth_a, forth_marks = back_inside(own_a), forth(own_a), forth(own_marks)
    left_a = turn(own_a)
    own_b, inside_a, forth_a, forth_marks, left_a = tied(own_b, inside_a, forth_a, forth_marks, left_a)
    near_b, crossed_a, far_a = back(own_b), last_crossed(inside_a), forth_last(forth_a)
    left_b = turn(own_b)
    forth_marks, left_b = tied(forth_marks, left_b)
    near_marks, far_marks = back(own_marks), forth_last(forth_marks)
    near_b, crossed_a, far_a, where = tied(near_b, crossed_a, far_a, copied(where))
    far_b = back(near_b)
    near_marks_pair = swapped(near_marks)
    own_pair_a, own_pair_b, inside_pair_a = swapped(own_a), swapped(own_b), swapped(inside_a)
    own_marks_pair, far_marks_pair = swapped(own_marks), swapped(far_marks)
    crossed_pair_a, near_pair_b, far_pair_a = swapped(crossed_a), swapped(near_b), swapped(far_a)
    weight = weights(where, own_marks, own_marks_pair, near_marks_pair, near_marks)
    far_weight = weights(where, own_marks, near_marks_pair, far_marks_pair, far_marks)
    jobs = [
        (left_b, deep, 1, [(near_b, None, None)]),
        (left_b, deep, 0, [(own_pair_b, 0, None), (near_pair_b, 1, None)]),
        (left_a, 0, 1, [(inside_a, None, 0), (crossed_a, None, 1)]),
        (left_a, 0, 0, [(own_pair_a, 0, None), (inside_pair_a, 1, 0), (crossed_pair_a, 1, 1)]),
    ]
    out = cross(where, weight, jobs, kept, None)
    jobs = [
        (left_a, 0, 3, [(far_a, None, None)]),
        (left_a, 0, 2, [(inside_pair_a, 0, 0), (crossed_pair_a, 0, 1), (far_pair_a, 1, None)]),
    ]
    out = cross(where, far_weight, jobs, kept, out)
    far_b, out = tied(far_b, out)
    far_pair_b = swapped(far_b)
    out = cross(where, far_weight, [(left_b, deep, 3, [(far_b, None, None)])], kept, out)
    return cross(where, far_weight, [(left_b, deep, 2, [(near_pair_b, 0, None), (far_pair_b, 1, None)])], kept, out)


def solution(mesh):
    return jax.shard_map(
        shards,
        mesh=mesh,
        in_specs=(P("bin", "blk", None, None), P("bin", "blk"), P()),
        out_specs=P(None, None, "bin", "blk", None),
        check_vma=False,
    )
```

```python
import jax
import jax.numpy as jnp
from jax import lax
from jax.experimental import pallas as pl
from jax.experimental.pallas import tpu as pltpu
from jax.sharding import PartitionSpec as P

FB = 128
HALF_SPAN = 4
ROUNDS = 4
ROWS_Z = 4
WIN_STEP = 8
WIN_GROUP = 16
PIECES = 2
CHUNKS = 2
MIB = 1024 * 1024
COST = 1000


def taking(micros):
    return pl.CostEstimate(flops=int(micros * COST), bytes_accessed=1000, transcendentals=0)


def whiten_kernel(bins_ref, x_ref, q_ref, *refs, channels, kept, shares, pieces):
    outs = refs[:pieces]
    parted, band, picker, staged, quality = refs[pieces:]
    depth = kept // shares // pieces
    step = pl.program_id(0)
    group = pl.multiple_of(step * WIN_STEP // WIN_GROUP * WIN_GROUP, WIN_GROUP)

    @pl.when(step == 0)
    def _():
        quality[...] = q_ref[...].astype(jnp.float32)
        lanes = lax.broadcasted_iota(jnp.int32, (kept, 2 * FB), 1)
        rows = lax.broadcasted_iota(jnp.int32, (kept, 2 * FB), 0)
        wanted = jnp.zeros((kept, 2 * FB), jnp.int32)
        for n in range(kept):
            wanted = jnp.where(rows == n, bins_ref[n], wanted)
        offset = jnp.where(lanes >= FB, lanes - FB, lanes)
        near = jnp.abs(offset - wanted) <= HALF_SPAN
        band[:kept] = jnp.where(near, 1.0, 0.0).astype(jnp.bfloat16)
        band[kept:] = jnp.ones((16, 2 * FB), jnp.bfloat16)
        exact = offset == wanted
        picker[:kept] = jnp.where(exact & (lanes < FB), 1.0, 0.0).astype(jnp.bfloat16)
        picker[kept:] = jnp.where(exact & (lanes >= FB), 1.0, 0.0).astype(jnp.bfloat16)

    along = (((1,), (1,)), ((), ()))
    for k in range(WIN_STEP):
        parted[k] = x_ref[k].astype(jnp.float32)
        real = parted[k, pl.ds(0, channels, stride=2), :]
        imag = parted[k, pl.ds(1, channels, stride=2), :]
        power = real * real + imag * imag
        high = power.astype(jnp.bfloat16)
        low = (power - high.astype(jnp.float32)).astype(jnp.bfloat16)
        sums = lax.dot_general(
            band[...], jnp.concatenate([high, low], 1), along, preferred_element_type=jnp.float32
        )
        picked = [
            lax.dot_general(
                picker[:kept, :FB], value.astype(jnp.bfloat16), along, preferred_element_type=jnp.float32
            )
            for value in (real, imag)
        ]
        level = sums[kept:kept + 1] * (0.1 / FB) + 1e-06
        scale = lax.rsqrt(sums[:kept] * (1.0 / (2 * HALF_SPAN + 1)) + level)
        window = step * WIN_STEP + k
        gain = quality[pl.ds(window, 1), :] * scale
        local = lax.rem(window, WIN_GROUP)
        value = jnp.concatenate([picked[0] * gain, picked[1] * gain], 0)
        for c in range(0, channels, 128):
            staged[c // 128, pl.ds(local, 2 * kept, stride=WIN_GROUP), :] = value[:, c:c + 128]

    @pl.when(lax.rem(step, WIN_GROUP // WIN_STEP) == WIN_GROUP // WIN_STEP - 1)
    def _():
        for n in range(kept):
            share, place = n // (kept // shares), n % (kept // shares)
            for part in range(2):
                row = (part * kept + n) * WIN_GROUP
                for c in range(0, channels, 128):
                    value = staged[c // 128, row:row + WIN_GROUP, :].astype(jnp.bfloat16)
                    outs[place // depth][share, place % depth * 2 + part, :, c:c + 128] = value
        for share in range(shares):
            outs[-1][share, 2 * depth] = q_ref[pl.ds(group, WIN_GROUP), :]


def whiten(spectra, quality, bins, shares):
    windows, channels = quality.shape
    kept = bins.shape[0]
    paired = spectra.reshape(windows, channels * 2, FB)
    group = WIN_GROUP // WIN_STEP
    depth = kept // shares // PIECES
    rows = [2 * depth + (place == PIECES - 1) for place in range(PIECES)]
    return pl.pallas_call(
        lambda *refs: whiten_kernel(*refs, channels=channels, kept=kept, shares=shares, pieces=PIECES),
        grid=(windows // WIN_STEP,),
        in_specs=[
            pl.BlockSpec(memory_space=pltpu.SMEM),
            pl.BlockSpec((WIN_STEP, channels * 2, FB), lambda i: (i, 0, 0)),
            pl.BlockSpec((windows, channels), lambda i: (0, 0)),
        ],
        out_specs=[pl.BlockSpec((shares, r, WIN_GROUP, channels), lambda i: (0, 0, i // group, 0)) for r in rows],
        out_shape=[jax.ShapeDtypeStruct((shares, r, windows, channels), jnp.bfloat16) for r in rows],
        scratch_shapes=[
            pltpu.VMEM((WIN_STEP, channels * 2, FB), jnp.float32),
            pltpu.VMEM((kept + 16, 2 * FB), jnp.bfloat16),
            pltpu.VMEM((2 * kept, 2 * FB), jnp.bfloat16),
            pltpu.VMEM((channels // 128, 2 * kept * WIN_GROUP, 128), jnp.float32),
            pltpu.VMEM((windows, channels), jnp.float32),
        ],
        compiler_params=pltpu.CompilerParams(vmem_limit_bytes=60 * MIB),
        cost_estimate=taking(11),
    )(bins, paired, quality)


def turn_kernel(own_ref, out_ref):
    channels = own_ref.shape[-1]
    depth = out_ref.shape[-1]
    own = own_ref[...]
    out_ref[:channels] = own.reshape(depth, channels).T
    turned = jnp.concatenate([own[:, 1:], -own[:, :1]], 1)
    out_ref[channels:] = turned.reshape(depth, channels).T


def turn(own):
    shares, rows, windows, channels = own.shape
    deep = rows // 2
    depth = shares * 2 * windows
    return pl.pallas_call(
        turn_kernel,
        grid=(deep,),
        in_specs=[pl.BlockSpec((shares, 2, windows, channels), lambda n: (0, n, 0, 0))],
        out_specs=pl.BlockSpec((None, 2 * channels, depth), lambda n: (n, 0, 0)),
        out_shape=jax.ShapeDtypeStruct((deep, 2 * channels, depth), jnp.bfloat16),
        compiler_params=pltpu.CompilerParams(vmem_limit_bytes=63 * MIB),
        cost_estimate=taking(1.5),
    )(own)


def weight_kernel(where_ref, own_ref, first_ref, second_ref, both_ref, out_ref):
    shares, _, windows, channels = own_ref.shape
    depth = shares * windows
    own = own_ref[...].reshape(depth, channels).T
    for r, other in enumerate([jnp.where(where_ref[0] == 0, first_ref[...], second_ref[...]), both_ref[...]]):
        counts = jnp.dot(own, other.reshape(depth, channels), preferred_element_type=jnp.float32)
        out_ref[r] = lax.rsqrt(jnp.maximum(counts, 1.0))


def weights(where, *marks):
    channels = marks[0].shape[-1]
    return pl.pallas_call(
        weight_kernel,
        grid=(1,),
        in_specs=[pl.BlockSpec(memory_space=pltpu.SMEM)]
        + [pl.BlockSpec(value.shape, lambda g: (0, 0, 0, 0)) for value in marks],
        out_specs=pl.BlockSpec((2, channels, channels), lambda g: (0, 0, 0)),
        out_shape=jax.ShapeDtypeStruct((2, channels, channels), jnp.float32),
        compiler_params=pltpu.CompilerParams(vmem_limit_bytes=16 * MIB),
        cost_estimate=taking(1),
    )(where, *marks)


def cross_kernel(where_ref, weight_ref, *refs, jobs, deep, rounds):
    out_ref = refs[-1]
    channels = out_ref.shape[-1]
    depth = refs[jobs[0][0]].shape[-1]
    job, n = pl.program_id(0) // deep, lax.rem(pl.program_id(0), deep)
    rows = channels // CHUNKS

    def products(left_ref, other_ref, r):
        other = other_ref[...].reshape(depth, channels)
        for part in range(2):
            for i in range(CHUNKS):
                left = left_ref[n if left_ref.shape[0] > 1 else 0, part * channels + i * rows:part * channels + (i + 1) * rows]
                product = jnp.dot(left, other, preferred_element_type=jnp.float32)
                weight = weight_ref[r, i * rows:(i + 1) * rows]
                out_ref[part, i * rows:(i + 1) * rows] = (product * weight).astype(jnp.bfloat16)

    for at, (left, _, r, sources) in enumerate(jobs):
        for place, (source, core, last) in enumerate(sources):
            wanted = job == at
            if core is not None:
                wanted = wanted & (where_ref[0] == core)
            if last is not None:
                wanted = wanted & (where_ref[1] == last)

            @pl.when(wanted)
            def _(left=left, source=source, r=r):
                products(refs[left], refs[source], r - rounds[0])


def cross(where, weight, jobs, kept, held):
    arrays, plan, first_job = [], [], []

    def put(value, job):
        for at, other in enumerate(arrays):
            if other is value:
                return at
        arrays.append(value)
        first_job.append(job)
        return len(arrays) - 1

    lefts = []
    for at, (left, place, r, choices) in enumerate(jobs):
        lefts.append(put(left, None))
    for at, (left, place, r, choices) in enumerate(jobs):
        plan.append((lefts[at], place, r, [(put(value, at), core, last) for value, core, last in choices]))
    deep, double, depth = jobs[0][0].shape
    channels = double // 2
    extra = [] if held is None else [held]
    used = sorted({r for _, _, r, _ in plan})
    rounds = (used[0] // 2 * 2, 2) if len(used) > 1 else (used[0], 1)

    def spec(value, job):
        if job is None:
            if len(plan) == 1:
                return pl.BlockSpec((1, double, depth), lambda g: (g, 0, 0))
            return pl.BlockSpec(value.shape, lambda g: (0, 0, 0), pipeline_mode=pl.Buffered(1))
        shares, _, windows, _ = value.shape
        return pl.BlockSpec(
            (shares, 2, windows, channels), lambda g: (0, jnp.clip(g - job * deep, 0, deep - 1), 0, 0)
        )

    def chosen(job, values):
        result = values[0]
        for at in range(1, len(values)):
            result = jnp.where(job == at, values[at], result)
        return result

    def target(g):
        job = g // deep
        place = chosen(job, [p[1] for p in plan]) + lax.rem(g, deep)
        return chosen(job, [p[2] for p in plan]), 0, place, 0, 0

    return pl.pallas_call(
        lambda *refs: cross_kernel(*refs, jobs=plan, deep=deep, rounds=rounds),
        grid=(len(plan) * deep,),
        in_specs=[pl.BlockSpec(memory_space=pltpu.SMEM)]
        + [
            pl.BlockSpec(
                (rounds[1], channels, channels), lambda g: (rounds[0] % 2 // rounds[1], 0, 0), pipeline_mode=pl.Buffered(1)
            )
        ]
        + [spec(value, job) for value, job in zip(arrays, first_job)]
        + [pl.BlockSpec(memory_space=pl.ANY)] * len(extra),
        out_specs=pl.BlockSpec((None, 2, None, channels, channels), target),
        out_shape=jax.ShapeDtypeStruct((ROUNDS, 2, kept, channels, channels), jnp.bfloat16),
        input_output_aliases={} if held is None else {2 + len(arrays): 0},
        compiler_params=pltpu.CompilerParams(vmem_limit_bytes=32 * MIB),
        cost_estimate=taking(1),
    )(where, weight, *arrays, *extra)


def copied_kernel(value_ref, out_ref):
    for at in range(value_ref.shape[0]):
        out_ref[at] = value_ref[at]


def copied(value):
    scalars = pl.BlockSpec(memory_space=pltpu.SMEM)
    return pl.pallas_call(
        copied_kernel,
        in_specs=[scalars],
        out_specs=scalars,
        out_shape=jax.ShapeDtypeStruct(value.shape, value.dtype),
        compiler_params=pltpu.CompilerParams(vmem_limit_bytes=63 * MIB),
        cost_estimate=taking(0.1),
    )(value)


def tied(*values):
    return lax.optimization_barrier(values)


def gate_kernel(value_ref, *refs):
    del value_ref, refs


def gated(value, *others):
    anywhere = pl.BlockSpec(memory_space=pl.ANY)
    return pl.pallas_call(
        gate_kernel,
        in_specs=[anywhere] * (1 + len(others)),
        out_specs=anywhere,
        out_shape=jax.ShapeDtypeStruct(value.shape, value.dtype),
        input_output_aliases={0: 0},
        cost_estimate=taking(0.1),
    )(value, *others)


def shards(spectra, quality, bins):
    blocks = lax.axis_size("blk")
    shares = lax.axis_size("bin")
    chips = blocks // 2
    block = lax.axis_index("blk")
    where = jnp.stack([block % 2, (block // 2 % ROWS_Z == ROWS_Z - 1).astype(jnp.int32)])

    def moved(value, pairs):
        return lax.ppermute(value, "blk", [(2 * s + c, 2 * t + c) for s, t in pairs for c in range(2)])

    def back(value):
        return moved(value, [((t + 1) % chips, t) for t in range(chips)])

    def chip(row, z):
        return (row % (chips // ROWS_Z)) * ROWS_Z + z % ROWS_Z

    every = [(row, z) for row in range(chips // ROWS_Z) for z in range(ROWS_Z)]

    def forth(value):
        return moved(value, [(chip(row, z - 1), chip(row, z)) for row, z in every])

    def forth_last(value):
        return moved(value, [(chip(row + (z + 2) // ROWS_Z, z - 1), chip(row, z)) for row, z in every])

    def swapped(value):
        return lax.ppermute(value, "blk", [(i, i ^ 1) for i in range(blocks)])

    def back_inside(value):
        return moved(value, [(chip(row, z + 1), chip(row, z)) for row, z in every])

    def last_crossed(value):
        rows = chips // ROWS_Z
        return moved(value, [(chip(row + 1, -1), chip(row, -1)) for row in range(rows)])

    def far_back(value):
        return moved(value, [((t + 2) % chips, t) for t in range(chips)])

    def to_bins(value):
        return lax.all_to_all(value, "bin", split_axis=0, concat_axis=0, tiled=True)

    kept = bins.shape[0] // shares
    deep = kept // PIECES
    sent_a, sent_b = whiten(spectra, quality, bins, shares)
    own_a = to_bins(sent_a)
    sent_b, own_a = tied(sent_b, own_a)
    own_all = to_bins(sent_b)
    own_b, own_marks = own_all[:, :2 * deep], own_all[:, 2 * deep:]
    inside_a, forth_a, forth_marks = back_inside(own_a), forth(own_a), forth(own_marks)
    left_a = turn(own_a)
    own_b, inside_a, forth_a, forth_marks, left_a = tied(own_b, inside_a, forth_a, forth_marks, left_a)
    near_b, crossed_a, far_a = back(own_b), last_crossed(inside_a), forth_last(forth_a)
    left_b = turn(own_b)
    forth_marks, left_b = tied(forth_marks, left_b)
    near_marks, far_marks = back(own_marks), forth_last(forth_marks)
    near_b, crossed_a, far_a, where = tied(near_b, crossed_a, far_a, copied(where))
    far_b = back(near_b)
    near_marks_pair = swapped(near_marks)
    own_pair_a, own_pair_b, inside_pair_a = swapped(own_a), swapped(own_b), swapped(inside_a)
    own_marks_pair, far_marks_pair = swapped(own_marks), swapped(far_marks)
    crossed_pair_a, near_pair_b, far_pair_a = swapped(crossed_a), swapped(near_b), swapped(far_a)
    weight = weights(where, own_marks, own_marks_pair, near_marks_pair, near_marks)
    far_weight = weights(where, own_marks, near_marks_pair, far_marks_pair, far_marks)
    jobs = [
        (left_b, deep, 1, [(near_b, None, None)]),
        (left_b, deep, 0, [(own_pair_b, 0, None), (near_pair_b, 1, None)]),
        (left_a, 0, 1, [(inside_a, None, 0), (crossed_a, None, 1)]),
        (left_a, 0, 0, [(own_pair_a, 0, None), (inside_pair_a, 1, 0), (crossed_pair_a, 1, 1)]),
    ]
    out = cross(where, weight, jobs, kept, None)
    jobs = [
        (left_a, 0, 3, [(far_a, None, None)]),
        (left_a, 0, 2, [(inside_pair_a, 0, 0), (crossed_pair_a, 0, 1), (far_pair_a, 1, None)]),
    ]
    out = cross(where, far_weight, jobs, kept, out)
    far_b, out = tied(far_b, out)
    far_pair_b = swapped(far_b)
    out = cross(where, far_weight, [(left_b, deep, 3, [(far_b, None, None)])], kept, out)
    return cross(where, far_weight, [(left_b, deep, 2, [(near_pair_b, 0, None), (far_pair_b, 1, None)])], kept, out)


def solution(mesh):
    return jax.shard_map(
        shards,
        mesh=mesh,
        in_specs=(P("bin", "blk", None, None), P("bin", "blk"), P()),
        out_specs=P(None, None, "bin", "blk", None),
        check_vma=False,
    )
```
